256 devices in a mesh: row: 8 (over z), col: 32 (over y, x, core).
Axes of the slice: x: 4, y: 4, z: 8, core: 2. Of those that a mesh axis runs over, the one named last changes fastest.
Arguments:
- diag_block: float32 [512, 512], P(('row', 'col')), may hold values from -1 to 140, as said below
- panel: float32 [12, 8, 32, 16, 512], P(None, 'row', 'col'), may hold values from -8 to 8
- slab: float32 [12, 8, 512, 32, 256], P(None, 'row', None, 'col'), may hold values from -6 to 6
Outputs:
- diag_factor: float32 [512, 512], P(('row', 'col'))
- panel_factor: float32 [12, 8, 32, 16, 512], P(None, 'row', 'col')
- new_slab: float32 [12, 8, 512, 32, 256], P(None, 'row', None, 'col')
The draws below stay inside these ranges and needn't reach their ends.
Inputs may be any that keep to these rules, and one draw needn't show every extreme that they name: diag_block is symmetric positive definite.
All inputs are finite; a program needn't handle non-finite values.
Results may differ from the reference program's by a relative error of at most 0.0003.
Values sent between devices are 32-bit elements; how exact they have to be, the bound alone decides.
No kernel may reach another device: no remote copies, remote signals or barrier semaphores. Data moves between devices by JAX's collectives and lax.ppermute only.
A program may use at most 128 MiB of HBM per device.

```python
import jax
import jax.numpy as jnp
from jax import lax

NB = 512
CYC = 12
CW = 256
RB = 16
TRAIL = 49152
WIN = 8192
N_ROW = 8
N_COL = 32


def draw_diag_block(key, part):
    key = jax.random.fold_in(key, 11)
    first, second, third = jax.random.split(key, 3)
    length = jax.random.uniform(third, (), jnp.float32, 3.5, 4.5)
    index = jnp.arange(NB, dtype=jnp.float32)
    distance = (index[:, None] - index[None, :]) / length
    kernel = 100.0 * jnp.exp(-0.5 * distance * distance)
    entries = jax.random.uniform(first, (NB, NB), jnp.float32, -0.5, 0.5)
    upper = jnp.triu(entries, 1)
    jitter = jax.random.uniform(second, (NB,), jnp.float32, 30.0, 40.0)
    return kernel + upper + upper.T + jnp.diag(jitter)


def steps_of(rng, shape, cuts, smallest, high):
    def one(axis_at, parts):
        draws = jax.random.uniform(jax.random.fold_in(jax.random.fold_in(rng, 6), axis_at), (parts,), jnp.float32, smallest / len(cuts), high / len(cuts))
        return jnp.repeat(jnp.exp(draws), shape[axis_at] // parts).reshape((-1,) + (1,) * (len(shape) - axis_at - 1))

    loudness = one(*cuts[0])
    for cut in cuts[1:]:
        loudness = loudness * one(*cut)
    return loudness


def centred(own_key, dims, spread, most, cuts=(), kind=jnp.bfloat16):
    values = spread * jax.random.normal(own_key, dims, jnp.float32)
    if cuts:
        values = values * steps_of(own_key, dims, cuts, -0.22, 0.18)
    return jnp.clip(values, -most, most).astype(kind)


def setup_inputs(seed: int = 0) -> dict:
    streams_of = jax.random.split(jax.random.key(seed), 4)
    return {
        "diag_block": draw_diag_block(jax.random.fold_in(streams_of[3], 71), 0),
        "panel": centred(streams_of[1], (CYC, N_ROW, N_COL, RB, NB), 2.0, 8.0, ((1, 8), (2, 32)), jnp.float32),
        "slab": centred(streams_of[2], (CYC, N_ROW, NB, N_COL, CW), 1.0, 6.0, ((1, 8), (3, 32)), jnp.float32),
    }


def reference(diag_block, panel, slab):
    diag_factor = jnp.linalg.cholesky(diag_block)
    identity = jnp.eye(NB, dtype=diag_block.dtype)
    inverse = jax.scipy.linalg.solve_triangular(diag_factor, identity, lower=True)
    rows = panel.reshape(TRAIL, NB)
    lower = jnp.dot(rows, inverse.T, precision=lax.Precision.HIGHEST)
    window = lower[:WIN]
    matrix = slab.reshape(TRAIL, WIN)
    updated = matrix - jnp.dot(lower, window.T, precision=lax.Precision.HIGHEST)
    return (diag_factor, lower.reshape(panel.shape), updated.reshape(slab.shape))
```

```python
import jax
import jax.numpy as jnp
import numpy as np
from jax import lax
from jax.experimental import pallas as pl
from jax.experimental.pallas import tpu as pltpu
from jax.sharding import Mesh, PartitionSpec as P

F32, BF16 = jnp.float32, jnp.bfloat16
NZ, NY, NX, NC = 8, 4, 4, 2
ALL = ("z", "y", "x", "core")
VMEM = pl.BlockSpec(memory_space=pltpu.VMEM)
HBM = pl.BlockSpec(memory_space=pl.ANY)
SMEM = pl.BlockSpec(memory_space=pltpu.SMEM)


def dot(a, b):
    return jnp.dot(a, b, precision=lax.Precision.HIGHEST, preferred_element_type=F32)


def dot_t(a, b):
    return lax.dot_general(
        a, b, (((1,), (1,)), ((), ())), precision=lax.Precision.HIGHEST, preferred_element_type=F32
    )


def row(v, j):
    return jnp.broadcast_to(v[j : j + 1, :], (8, 128))


def col(v, c):
    return jnp.broadcast_to(v[:, c : c + 1], (8, 128))


def factor_tile(read, tiles=16):
    sub = lax.broadcasted_iota(jnp.int32, (8, 128), 0)
    lane = lax.broadcasted_iota(jnp.int32, (8, 128), 1)
    left = [read(r) for r in range(tiles)]
    right = [jnp.where(lane == sub + 8 * r, 1.0, 0.0).astype(F32) for r in range(tiles)]
    up, inv = [], []
    for k in range(tiles):
        a, b = left[k], right[k]
        c = [col(a, 8 * k + j) for j in range(8)]
        ua = ub = dv = jnp.zeros((8, 128), F32)
        for j in range(8):
            at = sub == j
            piv = row(c[j], j)
            rec = 1.0 / piv
            ra, rb = row(a, j), row(b, j)
            ua, ub, dv = jnp.where(at, ra, ua), jnp.where(at, rb, ub), jnp.where(at, piv, dv)
            cj = c[j]
            for m in range(j + 1, 8):
                rm = row(c[m], j) * rec
                c[m] = jnp.where(at, rm, c[m] - cj * rm)
            ra, rb = ra * rec, rb * rec
            a, b = jnp.where(at, ra, a - cj * ra), jnp.where(at, rb, b - cj * rb)
        rs = lax.rsqrt(dv)
        up.append(jnp.where(lane >= sub + 8 * k, ua * rs, 0.0))
        inv.append(ub * rs)
        if k < tiles - 1:
            va, vb = [row(a, j) for j in range(8)], [row(b, j) for j in range(8)]
            for r in range(k + 1, tiles):
                cs = [col(left[r], 8 * k + j) for j in range(8)]

                def total(v, cs=cs):
                    p = [cs[j] * v[j] for j in range(8)]
                    return ((p[0] + p[1]) + (p[2] + p[3])) + ((p[4] + p[5]) + (p[6] + p[7]))

                left[r] = left[r] - total(va)
                right[r] = right[r] - total(vb)
    return jnp.concatenate(up, 0), jnp.concatenate(inv, 0)


def factor_kernel(a_ref, l_ref, i_ref, w):
    tiles = a_ref.shape[0] // 128
    w[...] = a_ref[...]
    l_ref[...] = jnp.zeros_like(l_ref)
    i_ref[...] = jnp.zeros_like(i_ref)
    for t in range(tiles):
        lo, hi = t * 128, (t + 1) * 128
        u, inv = factor_tile(lambda r: w[lo + 8 * r : lo + 8 * r + 8, lo:hi])
        l_ref[lo:hi, lo:hi] = u.T
        if t:
            i_ref[lo:hi, :lo] = dot(inv, i_ref[lo:hi, :lo])
        i_ref[lo:hi, lo:hi] = inv
        if t < tiles - 1:
            u12 = dot(inv, w[lo:hi, hi:])
            l21 = u12.T
            l_ref[hi:, lo:hi] = l21
            w[hi:, hi:] -= dot(l21, u12)
            i_ref[hi:, :hi] -= dot(l21, i_ref[lo:hi, :hi])


def factor_and_inverse(a):
    shape = jax.ShapeDtypeStruct(a.shape, F32)
    return pl.pallas_call(
        factor_kernel,
        out_shape=(shape, shape),
        in_specs=[VMEM],
        out_specs=(VMEM, VMEM),
        scratch_shapes=[pltpu.VMEM(a.shape, F32)],
        compiler_params=pltpu.CompilerParams(vmem_limit_bytes=24 << 20),
        cost_estimate=pl.CostEstimate(flops=20_000_000_000, bytes_accessed=3 << 20, transcendentals=0),
    )(a)


SLOTS = 3


def split(v):
    hi = v.astype(BF16)
    return hi, (v - hi.astype(F32)).astype(BF16)


def dot3(a, b):
    def one(p, q):
        return jnp.dot(p, q, preferred_element_type=F32)

    return one(a[0], b[0]) + (one(a[0], b[1]) + one(a[1], b[0]))


def update_kernel(where, inv, window, own, *refs):
    pieces, (s_ref, new_ref, mine_ref), (pb, sb, ob, whi, wlo, psem, ssem, osem) = refs[:-11], refs[-11:-8], refs[-8:]
    y, x, c = where[0], where[1], where[2]
    half_rows = s_ref.shape[0] // 2

    def coords(i):
        half, other, off = i // 8, (i // 4) % 2, i % 4
        return half, off, lax.rem(c + other, NC)

    def slab_part(ref, i, k):
        half, off, cc = coords(i)
        yy = lax.rem(y + off + half * (k - off), NY)
        xx = lax.rem(x + k + half * (off - k), NX)
        return ref.at[pl.ds(half * half_rows, half_rows), yy, xx, cc]

    def loads(i, slot, do):
        for k in range(NX):
            do(pltpu.make_async_copy(slab_part(s_ref, i, k), sb.at[slot, k], ssem.at[slot, k]))

    def piece_loads(i, slot, do):
        for n in range(16):
            parts = pieces[n]

            @pl.when(i == n)
            def _(parts=parts):
                at = 0
                for j, part in enumerate(parts):
                    size = part.shape[0]
                    do(pltpu.make_async_copy(part, pb.at[slot, pl.ds(at, size)], psem.at[slot, j]))
                    at += size

    def stores(i, slot, do):
        for k in range(NX):
            do(pltpu.make_async_copy(ob.at[slot, k], slab_part(new_ref, i, k), osem.at[slot, k]))

    def start(copy):
        copy.start()

    def wait(copy):
        copy.wait()

    for i in range(SLOTS - 1):
        loads(i, i, start)
        piece_loads(i, i, start)

    g = dot_t(window[...], inv[...])
    mine_ref[...] = dot_t(own[...], inv[...])
    w = dot(g, inv[...]).T
    whi[...], wlo[...] = split(w)

    @pl.loop(0, 16)
    def _(i):
        slot = lax.rem(i, SLOTS)

        @pl.when(i + SLOTS - 1 < 16)
        def _():
            later = lax.rem(i + SLOTS - 1, SLOTS)
            loads(i + SLOTS - 1, later, start)
            piece_loads(i + SLOTS - 1, later, start)

        loads(i, slot, wait)
        piece_loads(i, slot, wait)

        @pl.when(i >= SLOTS)
        def _():
            stores(i - SLOTS, slot, wait)

        got = dot3(split(pb[slot].reshape(-1, pb.shape[-1])), (whi[...], wlo[...]))
        ob[slot] = sb[slot] - got.reshape(ob.shape[1:])
        stores(i, slot, start)

    for i in range(16 - SLOTS, 16):
        stores(i, i % SLOTS, wait)


def update(where, inv, window, own, pieces, slab):
    flat = [a for parts in pieces for a in parts]
    sizes = [len(parts) for parts in pieces]
    cyc, width, order = slab.shape[0] // 2, slab.shape[-1], inv.shape[0]
    rb = slab.shape[-2]

    def body(where, inv, window, own, *refs):
        grouped, at = [], 0
        for n in sizes:
            grouped.append(refs[at : at + n])
            at += n
        update_kernel(where, inv, window, own, *grouped, *refs[at:])

    return pl.pallas_call(
        body,
        out_shape=(jax.ShapeDtypeStruct(slab.shape, F32), jax.ShapeDtypeStruct(own.shape, F32)),
        in_specs=[SMEM, VMEM, VMEM, VMEM] + [HBM] * (len(flat) + 1),
        out_specs=(HBM, VMEM),
        scratch_shapes=[
            pltpu.VMEM((SLOTS, NX, cyc, rb, order), F32),
            pltpu.VMEM((SLOTS, NX, cyc, rb, width), F32),
            pltpu.VMEM((SLOTS, NX, cyc, rb, width), F32),
            pltpu.VMEM((order, width), BF16),
            pltpu.VMEM((order, width), BF16),
            pltpu.SemaphoreType.DMA((SLOTS, 2)),
            pltpu.SemaphoreType.DMA((SLOTS, NX)),
            pltpu.SemaphoreType.DMA((SLOTS, NX)),
        ],
        compiler_params=pltpu.CompilerParams(vmem_limit_bytes=40 << 20),
        cost_estimate=pl.CostEstimate(flops=5_000_000_000, bytes_accessed=26 << 20, transcendentals=0),
    )(where, inv, window, own, *flat, slab)


def shift(v, axis, size, by):
    return lax.ppermute(v, axis, [((i + by) % size, i) for i in range(size)])


def other_core(v):
    return shift(v, "core", NC, 1)


def gather_diag(d):
    v = d.reshape(1, 1, 1, 1, *d.shape)
    for dim, (axis, size) in enumerate(zip(ALL, (NZ, NY, NX, NC))):
        step = 1
        while step < size:
            got = lax.ppermute(v, axis, [(i, i ^ step) for i in range(size)])
            upper = (lax.axis_index(axis) // step) % 2 == 1
            v = jnp.where(upper, jnp.concatenate([got, v], dim), jnp.concatenate([v, got], dim))
            step *= 2
    return v.reshape(-1, d.shape[-1])


def ring(v, axis, size=4):
    half = v.shape[0] // 2
    up, down = shift(v, axis, size, 1), shift(v, axis, size, -1)
    first = shift(down[:half], axis, size, -1)
    second = shift(up[half:], axis, size, 1)
    return [[v], [up], [first, second], [down]]


def local(diag_block, panel, slab):
    z, y, x, c = (lax.axis_index(a) for a in ALL)
    cyc, rb, order = panel.shape[0], panel.shape[-2], panel.shape[-1]
    p = panel.reshape(cyc, rb, order)
    whole = gather_diag(diag_block)

    first = ring(p[: cyc // 2], "x")
    block = jnp.stack([jnp.concatenate(b, 0) for b in first])
    half0 = ring(block, "y")
    second = ring(p[cyc // 2 :], "y")
    column = jnp.stack([jnp.concatenate(b, 0) for b in second])
    half1 = ring(column, "x")
    pieces = []
    for half in (half0, half1):
        pieces += half
        pieces += [[other_core(a) for a in parts] for parts in half]

    def of_cycle(parts):
        v = jnp.concatenate(parts, 0)
        return lax.dynamic_index_in_dim(v, y // 2, 1, False)

    held = [jnp.stack([of_cycle(parts) for parts in pieces[k : k + 4]]) for k in (0, 4)]
    mixed = jnp.stack([jnp.where(c == 0, held[0], held[1]), jnp.where(c == 0, held[1], held[0])], 2)
    mixed = jnp.roll(jnp.roll(mixed, x, 1), y, 0)
    wanted = lax.dynamic_slice_in_dim(mixed, 2 * c, 2, 0).reshape(-1, order)
    pairs = []
    for zz in range(NZ):
        for u in range(NZ):
            for cycle in range(2):
                for cc in range(NC):
                    to = lambda a, b: ((a * NY + 2 * cycle + b // NX) * NX + b % NX) * NC + cc
                    pairs.append((to(u, zz), to(zz, u)))
    window = lax.ppermute(wanted, ALL, pairs)

    factor, inverse = factor_and_inverse(whole)
    where = jnp.stack([y, x, c]).astype(jnp.int32)
    view = slab.reshape(cyc, NY, NX, NC, rb, slab.shape[-1])
    new, mine = update(where, inverse, window, p.reshape(-1, order), pieces, view)
    rows = diag_block.shape[0]
    index = ((z * NY + y) * NX + x) * NC + c
    own_factor = lax.dynamic_slice_in_dim(factor, index * rows, rows, 0)
    return own_factor, mine.reshape(panel.shape), new.reshape(slab.shape)


def solution(mesh):
    fine = Mesh(np.asarray(mesh.devices).reshape(NZ, NY, NX, NC), ALL)
    placed = (
        P(ALL, None),
        P(None, "z", ("y", "x", "core"), None, None),
        P(None, "z", None, ("y", "x", "core"), None),
    )
    return jax.shard_map(local, mesh=fine, in_specs=placed, out_specs=placed, check_vma=False)
```

```python
import jax
import jax.numpy as jnp
import numpy as np
from jax import lax
from jax.experimental import pallas as pl
from jax.experimental.pallas import tpu as pltpu
from jax.sharding import Mesh, PartitionSpec as P

F32, BF16 = jnp.float32, jnp.bfloat16
NZ, NY, NX, NC = 8, 4, 4, 2
ALL = ("z", "y", "x", "core")
VMEM = pl.BlockSpec(memory_space=pltpu.VMEM)
HBM = pl.BlockSpec(memory_space=pl.ANY)
SMEM = pl.BlockSpec(memory_space=pltpu.SMEM)


def dot(a, b):
    return jnp.dot(a, b, precision=lax.Precision.HIGHEST, preferred_element_type=F32)


def dot_t(a, b):
    return lax.dot_general(
        a, b, (((1,), (1,)), ((), ())), precision=lax.Precision.HIGHEST, preferred_element_type=F32
    )


def row(v, j):
    return jnp.broadcast_to(v[j : j + 1, :], (8, 128))


def col(v, c):
    return jnp.broadcast_to(v[:, c : c + 1], (8, 128))


def factor_tile(read, tiles=16):
    sub = lax.broadcasted_iota(jnp.int32, (8, 128), 0)
    lane = lax.broadcasted_iota(jnp.int32, (8, 128), 1)
    left = [read(r) for r in range(tiles)]
    right = [jnp.where(lane == sub + 8 * r, 1.0, 0.0).astype(F32) for r in range(tiles)]
    up, inv = [], []
    for k in range(tiles):
        a, b = left[k], right[k]
        c = [col(a, 8 * k + j) for j in range(8)]
        ua = ub = dv = jnp.zeros((8, 128), F32)
        for j in range(8):
            at = sub == j
            piv = row(c[j], j)
            rec = 1.0 / piv
            ra, rb = row(a, j), row(b, j)
            ua, ub, dv = jnp.where(at, ra, ua), jnp.where(at, rb, ub), jnp.where(at, piv, dv)
            cj = c[j]
            for m in range(j + 1, 8):
                rm = row(c[m], j) * rec
                c[m] = jnp.where(at, rm, c[m] - cj * rm)
            ra, rb = ra * rec, rb * rec
            a, b = jnp.where(at, ra, a - cj * ra), jnp.where(at, rb, b - cj * rb)
        rs = lax.rsqrt(dv)
        up.append(jnp.where(lane >= sub + 8 * k, ua * rs, 0.0))
        inv.append(ub * rs)
        if k < tiles - 1:
            va, vb = [row(a, j) for j in range(8)], [row(b, j) for j in range(8)]
            for r in range(k + 1, tiles):
                cs = [col(left[r], 8 * k + j) for j in range(8)]

                def total(v, cs=cs):
                    p = [cs[j] * v[j] for j in range(8)]
                    return ((p[0] + p[1]) + (p[2] + p[3])) + ((p[4] + p[5]) + (p[6] + p[7]))

                left[r] = left[r] - total(va)
                right[r] = right[r] - total(vb)
    return jnp.concatenate(up, 0), jnp.concatenate(inv, 0)


def factor_step(t, w, l_ref, i_ref):
    order = w.shape[0]
    lo, hi = t * 128, (t + 1) * 128
    u, inv = factor_tile(lambda r: w[lo + 8 * r : lo + 8 * r + 8, lo:hi])
    l_ref[lo:hi, lo:hi] = u.T
    if t:
        i_ref[lo:hi, :lo] = dot(inv, i_ref[lo:hi, :lo])
    i_ref[lo:hi, lo:hi] = inv
    if hi < order:
        u12 = dot(inv, w[lo:hi, hi:])
        l21 = u12.T
        l_ref[hi:, lo:hi] = l21
        w[hi:, hi:] -= dot(l21, u12)
        i_ref[hi:, :hi] -= dot(l21, i_ref[lo:hi, :hi])


def first_kernel(where, own_ref, other_ref, w, l_ref, i_ref, tiles_ref):
    c = where[3]
    order = w.shape[0]
    per = NZ * NY * NX
    for flip, ref in enumerate((own_ref, other_ref)):
        for n in range(per):
            device = n % NZ * (NY * NX * NC) + n // NZ * NC + (c ^ flip)
            tiles_ref[pl.ds(pl.multiple_of(device * 8, 8), 8), :] = ref[n]
    for t in range(order // 128):
        w[:, t * 128 : (t + 1) * 128] = tiles_ref[pl.ds(t, order, stride=order // 128), :]
    l_ref[...] = jnp.zeros_like(l_ref)
    i_ref[...] = jnp.zeros_like(i_ref)
    factor_step(0, w, l_ref, i_ref)


def factor_first(where, own, other, order):
    shape = jax.ShapeDtypeStruct((order, order), F32)
    return pl.pallas_call(
        first_kernel,
        out_shape=(shape,) * 3,
        in_specs=[SMEM, VMEM, VMEM],
        out_specs=(VMEM,) * 3,
        scratch_shapes=[pltpu.VMEM((order * order // 128, 128), F32)],
        compiler_params=pltpu.CompilerParams(vmem_limit_bytes=16 << 20),
        cost_estimate=pl.CostEstimate(flops=6_000_000_000, bytes_accessed=3 << 20, transcendentals=0),
    )(where, own, other)


def factor_next(t, state):
    def body(w_in, l_in, i_in, w, l_ref, i_ref):
        factor_step(t, w, l_ref, i_ref)

    return pl.pallas_call(
        body,
        out_shape=tuple(jax.ShapeDtypeStruct(a.shape, F32) for a in state),
        in_specs=[VMEM] * 3,
        out_specs=(VMEM,) * 3,
        input_output_aliases={0: 0, 1: 1, 2: 2},
        compiler_params=pltpu.CompilerParams(vmem_limit_bytes=16 << 20),
        cost_estimate=pl.CostEstimate(flops=6_000_000_000, bytes_accessed=3 << 20, transcendentals=0),
    )(*state)


SLOTS = 3


def split(v):
    hi = v.astype(BF16)
    return hi, (v - hi.astype(F32)).astype(BF16)


def dot3(a, b):
    def one(p, q):
        return jnp.dot(p, q, preferred_element_type=F32)

    return one(a[0], b[0]) + (one(a[0], b[1]) + one(a[1], b[0]))


def update_kernel(where, inv, near, far, own, *refs):
    pieces, (s_ref, new_ref, mine_ref), (pb, sb, ob, win, whi, wlo, psem, ssem, osem) = refs[:-12], refs[-12:-9], refs[-9:]
    y, x, c = where[1], where[2], where[3]
    count = len(pieces)

    def slab_part(ref, i, k):
        core, off = lax.rem(c + i // 4, NC), lax.rem(i, 4)
        yy = lax.rem(y + off + core * (k - off), NY)
        xx = lax.rem(x + k + core * (off - k), NX)
        return ref.at[:, yy, xx, core]

    def loads(i, slot, do):
        for k in range(NX):
            do(pltpu.make_async_copy(slab_part(s_ref, i, k), sb.at[slot, k], ssem.at[slot, k]))

    def piece_loads(i, slot, do):
        for n in range(count):
            parts = pieces[n]

            @pl.when(i == n)
            def _(parts=parts):
                at = 0
                for j, part in enumerate(parts):
                    size = part.shape[0]
                    do(pltpu.make_async_copy(part, pb.at[slot, pl.ds(at, size)], psem.at[slot, j]))
                    at += size

    def stores(i, slot, do):
        for k in range(NX):
            do(pltpu.make_async_copy(ob.at[slot, k], slab_part(new_ref, i, k), osem.at[slot, k]))

    def start(copy):
        copy.start()

    def wait(copy):
        copy.wait()

    for i in range(SLOTS - 1):
        loads(i, i, start)
        piece_loads(i, i, start)

    part = near.shape[1]
    for n in range(NZ):
        v = near[n] if n < NZ // 2 else far[n - NZ // 2]
        bits = n % 2 * 4 + n // 2 % 2 * 2 + n // 4
        win[pl.ds(pl.multiple_of((where[0] ^ bits) * part, part), part), :] = v
    g = dot_t(win[...], inv[...])
    mine_ref[...] = dot_t(own[...], inv[...])
    w = dot(g, inv[...]).T
    whi[...], wlo[...] = split(w)

    @pl.loop(0, count)
    def _(i):
        slot = lax.rem(i, SLOTS)

        @pl.when(i + SLOTS - 1 < count)
        def _():
            later = lax.rem(i + SLOTS - 1, SLOTS)
            loads(i + SLOTS - 1, later, start)
            piece_loads(i + SLOTS - 1, later, start)

        loads(i, slot, wait)
        piece_loads(i, slot, wait)

        @pl.when(i >= SLOTS)
        def _():
            stores(i - SLOTS, slot, wait)

        got = dot3(split(pb[slot]), (whi[...], wlo[...]))
        rows = got.shape[0]
        old, new = sb.at[slot].reshape(2 * rows, 128), ob.at[slot].reshape(2 * rows, 128)
        for h in range(2):
            at = pl.ds(h, rows, stride=2)
            new[at, :] = old[at, :] - got[:, h * 128 : (h + 1) * 128]
        stores(i, slot, start)

    for i in range(count - SLOTS, count):
        stores(i, i % SLOTS, wait)


def update(where, inv, window, own, pieces, slab):
    flat = [a for parts in pieces for a in parts]
    sizes = [len(parts) for parts in pieces]
    cyc, rb, order = slab.shape[0], slab.shape[-2] // 2, inv.shape[0]
    width = slab.shape[-1] * 2

    def body(where, inv, near, far, own, *refs):
        grouped, at = [], 0
        for n in sizes:
            grouped.append(refs[at : at + n])
            at += n
        update_kernel(where, inv, near, far, own, *grouped, *refs[at:])

    return pl.pallas_call(
        body,
        out_shape=(jax.ShapeDtypeStruct(slab.shape, F32), jax.ShapeDtypeStruct(own.shape, F32)),
        in_specs=[SMEM, VMEM, VMEM, VMEM, VMEM] + [HBM] * (len(flat) + 1),
        out_specs=(HBM, VMEM),
        scratch_shapes=[
            pltpu.VMEM((SLOTS, NX * cyc * rb, order), F32),
            pltpu.VMEM((SLOTS, NX, cyc, 2 * rb, width // 2), F32),
            pltpu.VMEM((SLOTS, NX, cyc, 2 * rb, width // 2), F32),
            pltpu.VMEM((width, order), F32),
            pltpu.VMEM((order, width), BF16),
            pltpu.VMEM((order, width), BF16),
            pltpu.SemaphoreType.DMA((SLOTS, 2)),
            pltpu.SemaphoreType.DMA((SLOTS, NX)),
            pltpu.SemaphoreType.DMA((SLOTS, NX)),
        ],
        compiler_params=pltpu.CompilerParams(vmem_limit_bytes=40 << 20),
        cost_estimate=pl.CostEstimate(flops=5_000_000_000, bytes_accessed=26 << 20, transcendentals=0),
    )(where, inv, *window, own, *flat, slab)


def index(z, y, x, c):
    return ((z * NY + y) * NX + x) * NC + c


def receive(v, source):
    places = np.ndindex(NZ, NY, NX, NC)
    return lax.ppermute(v, ALL, [(index(*source(*at)), index(*at)) for at in places])


def along(phase, move):
    def source(z, y, x, c):
        return (z, y, move(x), c) if c == phase else (z, move(y), x, c)

    return source


def other_core(v):
    return receive(v, lambda z, y, x, c: (z, y, x, 1 - c))


def forward(up, down, phase):
    half = up.shape[0] // 2
    return [receive(down[:half], minus(phase)), receive(up[half:], plus(phase))]


def plus(phase):
    return along(phase, lambda i: (i + 1) % 4)


def minus(phase):
    return along(phase, lambda i: (i + 3) % 4)


def scatter(v, rows):
    core = lax.axis_index("core")
    got = other_core(v)
    sent = jnp.concatenate([jnp.where(core == 0, v[:rows], got[rows:]), jnp.where(core == 0, got[:rows], v[rows:])], 0)
    return receive(sent, lambda z, y, x, c: (y % 2 * NX + x, 2 * c + z // NX, z % NX, y // 2))


def everyone(v, axis, size):
    return lax.all_to_all(jnp.broadcast_to(v[None], (size, *v.shape)), axis, 0, 0, tiled=True)


def flip_z(b):
    return lambda z, y, x, c: (z ^ b, y, x, c)


def doubled(v, step):
    return jnp.concatenate([v, receive(v, step)], 0)


def local(diag_block, panel, slab):
    z, y, x, c = (lax.axis_index(a) for a in ALL)
    where = jnp.stack([z, y, x, c]).astype(jnp.int32)
    cyc, rb, order = panel.shape[0], panel.shape[-2], panel.shape[-1]
    p = own = panel.reshape(cyc * rb, order)
    tie = lax.optimization_barrier

    up, down = receive(p, plus(0)), receive(p, minus(0))
    d = everyone(diag_block.reshape(8, 128), "z", NZ)
    d, up, down = tie((d, up, down))
    first, second = forward(up, down, 0)
    block = jnp.concatenate([p, up, first, second, down], 0)
    up, down = receive(block, plus(1)), receive(block, minus(1))
    d = everyone(d, ("y", "x"), NY * NX).reshape(-1, 8, 128)
    w = scatter(p[: 2 * rb], rb).reshape(1, 2 * rb, order)
    other_block = other_core(block)
    d, w, other_block, up, down = tie((d, w, other_block, up, down))
    first, second = forward(up, down, 1)
    state = factor_first(where, d, other_core(d), order)
    w = doubled(w, flip_z(4))
    for t, bit in ((1, 2), (2, 1)):
        state, w = tie((state, w))
        got = receive(w, flip_z(bit))
        state = factor_next(t, state)
        if t == 1:
            w = jnp.concatenate([w, got], 0)
    state = factor_next(3, state)
    _, factor, inverse = state
    window = (w, got)
    pieces = [[block], [up], [first, second], [down]]
    pieces += [[other_block]] + [[other_core(a) for a in parts] for parts in pieces[1:]]

    view = slab.reshape(cyc, NY, NX, NC, 2 * rb, slab.shape[-1] // 2)
    new, mine = update(where, inverse, window, own, pieces, view)
    rows = diag_block.shape[0]
    own_factor = lax.dynamic_slice_in_dim(factor, index(z, y, x, c) * rows, rows, 0)
    return own_factor, mine.reshape(panel.shape), new.reshape(slab.shape)


def solution(mesh):
    fine = Mesh(np.asarray(mesh.devices).reshape(NZ, NY, NX, NC), ALL)
    placed = (
        P(ALL, None),
        P(None, "z", ("y", "x", "core"), None, None),
        P(None, "z", None, ("y", "x", "core"), None),
    )
    return jax.shard_map(local, mesh=fine, in_specs=placed, out_specs=placed, check_vma=False)
```

```python
import jax
import jax.numpy as jnp
import numpy as np
from jax import lax
from jax.experimental import pallas as pl
from jax.experimental.pallas import tpu as pltpu
from jax.sharding import Mesh, PartitionSpec as P

F32, BF16 = jnp.float32, jnp.bfloat16
NZ, NY, NX, NC = 8, 4, 4, 2
ALL = ("z", "y", "x", "core")
VMEM = pl.BlockSpec(memory_space=pltpu.VMEM)
HBM = pl.BlockSpec(memory_space=pl.ANY)
SMEM = pl.BlockSpec(memory_space=pltpu.SMEM)


def dot(a, b):
    return jnp.dot(a, b, precision=lax.Precision.HIGHEST, preferred_element_type=F32)


def dot_t(a, b):
    return lax.dot_general(
        a, b, (((1,), (1,)), ((), ())), precision=lax.Precision.HIGHEST, preferred_element_type=F32
    )


def row(v, j):
    return jnp.broadcast_to(v[j : j + 1, :], (8, 128))


def col(v, c):
    return jnp.broadcast_to(v[:, c : c + 1], (8, 128))


def factor_tile(read, tiles=16):
    sub = lax.broadcasted_iota(jnp.int32, (8, 128), 0)
    lane = lax.broadcasted_iota(jnp.int32, (8, 128), 1)
    left = [read(r) for r in range(tiles)]
    right = [jnp.where(lane == sub + 8 * r, 1.0, 0.0).astype(F32) for r in range(tiles)]
    up, inv = [], []
    for k in range(tiles):
        a, b = left[k], right[k]
        c = [col(a, 8 * k + j) for j in range(8)]
        ua = ub = dv = jnp.zeros((8, 128), F32)
        for j in range(8):
            at = sub == j
            piv = row(c[j], j)
            rec = 1.0 / piv
            ra, rb = row(a, j), row(b, j)
            ua, ub, dv = jnp.where(at, ra, ua), jnp.where(at, rb, ub), jnp.where(at, piv, dv)
            cj = c[j]
            for m in range(j + 1, 8):
                rm = row(c[m], j) * rec
                c[m] = jnp.where(at, rm, c[m] - cj * rm)
            ra, rb = ra * rec, rb * rec
            a, b = jnp.where(at, ra, a - cj * ra), jnp.where(at, rb, b - cj * rb)
        rs = lax.rsqrt(dv)
        up.append(jnp.where(lane >= sub + 8 * k, ua * rs, 0.0))
        inv.append(ub * rs)
        if k < tiles - 1:
            va, vb = [row(a, j) for j in range(8)], [row(b, j) for j in range(8)]
            for r in range(k + 1, tiles):
                cs = [col(left[r], 8 * k + j) for j in range(8)]

                def total(v, cs=cs):
                    p = [cs[j] * v[j] for j in range(8)]
                    return ((p[0] + p[1]) + (p[2] + p[3])) + ((p[4] + p[5]) + (p[6] + p[7]))

                left[r] = left[r] - total(va)
                right[r] = right[r] - total(vb)
    return jnp.concatenate(up, 0), jnp.concatenate(inv, 0)


def factor_step(t, w, l_ref, i_ref):
    order = w.shape[0]
    lo, hi = t * 128, (t + 1) * 128
    u, inv = factor_tile(lambda r: w[lo + 8 * r : lo + 8 * r + 8, lo:hi])
    l_ref[lo:hi, lo:hi] = u.T
    if t:
        i_ref[lo:hi, :lo] = dot(inv, i_ref[lo:hi, :lo])
    i_ref[lo:hi, lo:hi] = inv
    if hi < order:
        u12 = dot(inv, w[lo:hi, hi:])
        l21 = u12.T
        l_ref[hi:, lo:hi] = l21
        w[hi:, hi:] -= dot(l21, u12)
        i_ref[hi:, :hi] -= dot(l21, i_ref[lo:hi, :hi])


def first_kernel(where, own_ref, other_ref, w, l_ref, i_ref, tiles_ref):
    c = where[3]
    order = w.shape[0]
    per = NZ * NY * NX
    for flip, ref in enumerate((own_ref, other_ref)):
        for n in range(per):
            device = n % NZ * (NY * NX * NC) + n // NZ * NC + (c ^ flip)
            tiles_ref[pl.ds(pl.multiple_of(device * 8, 8), 8), :] = ref[n]
    for t in range(order // 128):
        w[:, t * 128 : (t + 1) * 128] = tiles_ref[pl.ds(t, order, stride=order // 128), :]
    l_ref[...] = jnp.zeros_like(l_ref)
    i_ref[...] = jnp.zeros_like(i_ref)
    factor_step(0, w, l_ref, i_ref)


def factor_first(where, own, other, order):
    shape = jax.ShapeDtypeStruct((order, order), F32)
    return pl.pallas_call(
        first_kernel,
        out_shape=(shape,) * 3,
        in_specs=[SMEM, VMEM, VMEM],
        out_specs=(VMEM,) * 3,
        scratch_shapes=[pltpu.VMEM((order * order // 128, 128), F32)],
        compiler_params=pltpu.CompilerParams(vmem_limit_bytes=16 << 20),
        cost_estimate=pl.CostEstimate(flops=6_000_000_000, bytes_accessed=3 << 20, transcendentals=0),
    )(where, own, other)


def factor_next(t, state):
    def body(w_in, l_in, i_in, w, l_ref, i_ref):
        factor_step(t, w, l_ref, i_ref)

    return pl.pallas_call(
        body,
        out_shape=tuple(jax.ShapeDtypeStruct(a.shape, F32) for a in state),
        in_specs=[VMEM] * 3,
        out_specs=(VMEM,) * 3,
        input_output_aliases={0: 0, 1: 1, 2: 2},
        compiler_params=pltpu.CompilerParams(vmem_limit_bytes=16 << 20),
        cost_estimate=pl.CostEstimate(flops=6_000_000_000, bytes_accessed=3 << 20, transcendentals=0),
    )(*state)


SLOTS = 3


def split(v):
    hi = v.astype(BF16)
    return hi, (v - hi.astype(F32)).astype(BF16)


def dot3(a, b):
    def one(p, q):
        return jnp.dot(p, q, preferred_element_type=F32)

    return one(a[0], b[0]) + (one(a[0], b[1]) + one(a[1], b[0]))


def update_kernel(where, inv, near, far, own, *refs):
    pieces, (s_ref, new_ref, mine_ref), (pb, sb, ob, win, whi, wlo, psem, ssem, osem) = refs[:-12], refs[-12:-9], refs[-9:]
    y, x, c = where[1], where[2], where[3]
    count = len(pieces)

    def slab_part(ref, i, k):
        core, off = lax.rem(c + i // 4, NC), lax.rem(i, 4)
        yy = lax.rem(y + off + core * (k - off), NY)
        xx = lax.rem(x + k + core * (off - k), NX)
        return ref.at[:, yy, xx, core]

    def loads(i, slot, do):
        for k in range(NX):
            do(pltpu.make_async_copy(slab_part(s_ref, i, k), sb.at[slot, k], ssem.at[slot, k]))

    def piece_loads(i, slot, do):
        for n in range(count):
            parts = pieces[n]

            @pl.when(i == n)
            def _(parts=parts):
                at = 0
                for j, part in enumerate(parts):
                    size = part.shape[0]
                    do(pltpu.make_async_copy(part, pb.at[slot, pl.ds(at, size)], psem.at[slot, j]))
                    at += size

    def stores(i, slot, do):
        for k in range(NX):
            do(pltpu.make_async_copy(ob.at[slot, k], slab_part(new_ref, i, k), osem.at[slot, k]))

    def start(copy):
        copy.start()

    def wait(copy):
        copy.wait()

    for i in range(SLOTS - 1):
        loads(i, i, start)
        piece_loads(i, i, start)

    part = near.shape[1]
    for n in range(NZ):
        v = near[n] if n < NZ // 2 else far[n - NZ // 2]
        bits = n % 2 * 4 + n // 2 % 2 * 2 + n // 4
        win[pl.ds(pl.multiple_of((where[0] ^ bits) * part, part), part), :] = v
    g = dot_t(win[...], inv[...])
    mine_ref[...] = dot_t(own[...], inv[...])
    w = dot(g, inv[...]).T
    whi[...], wlo[...] = split(w)

    @pl.loop(0, count)
    def _(i):
        slot = lax.rem(i, SLOTS)

        @pl.when(i + SLOTS - 1 < count)
        def _():
            later = lax.rem(i + SLOTS - 1, SLOTS)
            loads(i + SLOTS - 1, later, start)
            piece_loads(i + SLOTS - 1, later, start)

        loads(i, slot, wait)
        piece_loads(i, slot, wait)

        @pl.when(i >= SLOTS)
        def _():
            stores(i - SLOTS, slot, wait)

        got = dot3(split(pb[slot]), (whi[...], wlo[...]))
        rows = got.shape[0]
        old, new = sb.at[slot].reshape(2 * rows, 128), ob.at[slot].reshape(2 * rows, 128)
        for h in range(2):
            at = pl.ds(h, rows, stride=2)
            new[at, :] = old[at, :] - got[:, h * 128 : (h + 1) * 128]
        stores(i, slot, start)

    for i in range(count - SLOTS, count):
        stores(i, i % SLOTS, wait)


def update(where, inv, window, own, pieces, slab):
    flat = [a for parts in pieces for a in parts]
    sizes = [len(parts) for parts in pieces]
    cyc, rb, order = slab.shape[0], slab.shape[-2] // 2, inv.shape[0]
    width = slab.shape[-1] * 2

    def body(where, inv, near, far, own, *refs):
        grouped, at = [], 0
        for n in sizes:
            grouped.append(refs[at : at + n])
            at += n
        update_kernel(where, inv, near, far, own, *grouped, *refs[at:])

    return pl.pallas_call(
        body,
        out_shape=(jax.ShapeDtypeStruct(slab.shape, F32), jax.ShapeDtypeStruct(own.shape, F32)),
        in_specs=[SMEM, VMEM, VMEM, VMEM, VMEM] + [HBM] * (len(flat) + 1),
        out_specs=(HBM, VMEM),
        scratch_shapes=[
            pltpu.VMEM((SLOTS, NX * cyc * rb, order), F32),
            pltpu.VMEM((SLOTS, NX, cyc, 2 * rb, width // 2), F32),
            pltpu.VMEM((SLOTS, NX, cyc, 2 * rb, width // 2), F32),
            pltpu.VMEM((width, order), F32),
            pltpu.VMEM((order, width), BF16),
            pltpu.VMEM((order, width), BF16),
            pltpu.SemaphoreType.DMA((SLOTS, 2)),
            pltpu.SemaphoreType.DMA((SLOTS, NX)),
            pltpu.SemaphoreType.DMA((SLOTS, NX)),
        ],
        compiler_params=pltpu.CompilerParams(vmem_limit_bytes=40 << 20),
        cost_estimate=pl.CostEstimate(flops=5_000_000_000, bytes_accessed=26 << 20, transcendentals=0),
    )(where, inv, *window, own, *flat, slab)


def index(z, y, x, c):
    return ((z * NY + y) * NX + x) * NC + c


def receive(v, source):
    places = np.ndindex(NZ, NY, NX, NC)
    return lax.ppermute(v, ALL, [(index(*source(*at)), index(*at)) for at in places])


def along(phase, move):
    def source(z, y, x, c):
        return (z, y, move(x), c) if c == phase else (z, move(y), x, c)

    return source


def other_core(v):
    return receive(v, lambda z, y, x, c: (z, y, x, 1 - c))


def forward(up, down, phase):
    half = up.shape[0] // 2
    return [receive(down[:half], minus(phase)), receive(up[half:], plus(phase))]


def plus(phase):
    return along(phase, lambda i: (i + 1) % 4)


def minus(phase):
    return along(phase, lambda i: (i + 3) % 4)


def scatter(v, rows):
    core = lax.axis_index("core")
    got = other_core(v)
    sent = jnp.concatenate([jnp.where(core == 0, v[:rows], got[rows:]), jnp.where(core == 0, got[:rows], v[rows:])], 0)
    return receive(sent, lambda z, y, x, c: (y % 2 * NX + x, 2 * c + z // NX, z % NX, y // 2))


def everyone(v, axis, size):
    return lax.all_to_all(jnp.broadcast_to(v[None], (size, *v.shape)), axis, 0, 0, tiled=True)


def flip_z(b):
    return lambda z, y, x, c: (z ^ b, y, x, c)


def doubled(v, step):
    return jnp.concatenate([v, receive(v, step)], 0)


def local(diag_block, panel, slab):
    z, y, x, c = (lax.axis_index(a) for a in ALL)
    where = jnp.stack([z, y, x, c]).astype(jnp.int32)
    cyc, rb, order = panel.shape[0], panel.shape[-2], panel.shape[-1]
    p = own = panel.reshape(cyc * rb, order)
    tie = lax.optimization_barrier

    up, down = receive(p, plus(0)), receive(p, minus(0))
    d = everyone(diag_block.reshape(8, 128), "z", NZ)
    d, up, down = tie((d, up, down))
    first, second = forward(up, down, 0)
    block = jnp.concatenate([p, up, first, second, down], 0)
    d = everyone(d, ("y", "x"), NY * NX).reshape(-1, 8, 128)
    w = scatter(p[: 2 * rb], rb).reshape(1, 2 * rb, order)
    d, block = tie((d, block))
    up, down = receive(block, plus(1)), receive(block, minus(1))
    state = factor_first(where, d, other_core(d), order)
    for t, bit in ((1, 4), (2, 2), (3, 1)):
        if t == 2:
            state, w, up, down = tie((state, w, up, down))
            first, second = forward(up, down, 1)
        else:
            state, w = tie((state, w))
        got = receive(w, flip_z(bit))
        state = factor_next(t, state)
        if bit > 1:
            w = jnp.concatenate([w, got], 0)
    _, factor, inverse = state
    window = (w, got)
    pieces = [[block], [up], [first, second], [down]]
    pieces += [[other_core(a) for a in parts] for parts in pieces]

    view = slab.reshape(cyc, NY, NX, NC, 2 * rb, slab.shape[-1] // 2)
    new, mine = update(where, inverse, window, own, pieces, view)
    rows = diag_block.shape[0]
    own_factor = lax.dynamic_slice_in_dim(factor, index(z, y, x, c) * rows, rows, 0)
    return own_factor, mine.reshape(panel.shape), new.reshape(slab.shape)


def solution(mesh):
    fine = Mesh(np.asarray(mesh.devices).reshape(NZ, NY, NX, NC), ALL)
    placed = (
        P(ALL, None),
        P(None, "z", ("y", "x", "core"), None, None),
        P(None, "z", None, ("y", "x", "core"), None),
    )
    return jax.shard_map(local, mesh=fine, in_specs=placed, out_specs=placed, check_vma=False)
```

```python
import jax
import jax.numpy as jnp
import numpy as np
from jax import lax
from jax.experimental import pallas as pl
from jax.experimental.pallas import tpu as pltpu
from jax.sharding import Mesh, PartitionSpec as P

F32, BF16 = jnp.float32, jnp.bfloat16
NZ, NY, NX, NC = 8, 4, 4, 2
ALL = ("z", "y", "x", "core")
VMEM = pl.BlockSpec(memory_space=pltpu.VMEM)
HBM = pl.BlockSpec(memory_space=pl.ANY)
SMEM = pl.BlockSpec(memory_space=pltpu.SMEM)


def dot(a, b):
    return jnp.dot(a, b, precision=lax.Precision.HIGHEST, preferred_element_type=F32)


def row(v, j):
    return jnp.broadcast_to(v[j : j + 1, :], (8, 128))


def col(v, c):
    return jnp.broadcast_to(v[:, c : c + 1], (8, 128))


def factor_tile(read, tiles=16):
    sub = lax.broadcasted_iota(jnp.int32, (8, 128), 0)
    lane = lax.broadcasted_iota(jnp.int32, (8, 128), 1)
    left = [read(r) for r in range(tiles)]
    right = [jnp.where(lane == sub + 8 * r, 1.0, 0.0).astype(F32) for r in range(tiles)]
    up, inv = [], []
    for k in range(tiles):
        a, b = left[k], right[k]
        c = [col(a, 8 * k + j) for j in range(8)]
        ua = ub = dv = jnp.zeros((8, 128), F32)
        for j in range(8):
            at = sub == j
            piv = row(c[j], j)
            rec = 1.0 / piv
            ra, rb = row(a, j), row(b, j)
            ua, ub, dv = jnp.where(at, ra, ua), jnp.where(at, rb, ub), jnp.where(at, piv, dv)
            cj = c[j]
            for m in range(j + 1, 8):
                rm = row(c[m], j) * rec
                c[m] = jnp.where(at, rm, c[m] - cj * rm)
            ra, rb = ra * rec, rb * rec
            a, b = jnp.where(at, ra, a - cj * ra), jnp.where(at, rb, b - cj * rb)
        rs = lax.rsqrt(dv)
        up.append(jnp.where(lane >= sub + 8 * k, ua * rs, 0.0))
        inv.append(ub * rs)
        if k < tiles - 1:
            va, vb = [row(a, j) for j in range(8)], [row(b, j) for j in range(8)]
            for r in range(k + 1, tiles):
                cs = [col(left[r], 8 * k + j) for j in range(8)]

                def total(v, cs=cs):
                    p = [cs[j] * v[j] for j in range(8)]
                    return ((p[0] + p[1]) + (p[2] + p[3])) + ((p[4] + p[5]) + (p[6] + p[7]))

                left[r] = left[r] - total(va)
                right[r] = right[r] - total(vb)
    return jnp.concatenate(up, 0), jnp.concatenate(inv, 0)


def factor_step(t, w, l_ref, i_ref):
    order = w.shape[0]
    lo, hi = t * 128, (t + 1) * 128
    u, inv = factor_tile(lambda r: w[lo + 8 * r : lo + 8 * r + 8, lo:hi])
    l_ref[lo:hi, lo:hi] = u.T
    if t:
        i_ref[lo:hi, :lo] = dot(inv, i_ref[lo:hi, :lo])
    i_ref[lo:hi, lo:hi] = inv
    if hi < order:
        u12 = dot(inv, w[lo:hi, hi:])
        l21 = u12.T
        l_ref[hi:, lo:hi] = l21
        w[hi:, hi:] -= dot(l21, u12)
        i_ref[hi:, :hi] -= dot(l21, i_ref[lo:hi, :hi])


def first_kernel(where, own_ref, other_ref, w, l_ref, i_ref, tiles_ref):
    c = where[3]
    order = w.shape[0]
    per = NZ * NY * NX
    for flip, ref in enumerate((own_ref, other_ref)):
        for n in range(per):
            device = n % NZ * (NY * NX * NC) + n // NZ * NC + (c ^ flip)
            tiles_ref[pl.ds(pl.multiple_of(device * 8, 8), 8), :] = ref[n]
    for t in range(order // 128):
        w[:, t * 128 : (t + 1) * 128] = tiles_ref[pl.ds(t, order, stride=order // 128), :]
    l_ref[...] = jnp.zeros_like(l_ref)
    i_ref[...] = jnp.zeros_like(i_ref)
    factor_step(0, w, l_ref, i_ref)


def factor_first(where, own, other, order):
    shape = jax.ShapeDtypeStruct((order, order), F32)
    return pl.pallas_call(
        first_kernel,
        out_shape=(shape,) * 3,
        in_specs=[SMEM, VMEM, VMEM],
        out_specs=(VMEM,) * 3,
        scratch_shapes=[pltpu.VMEM((order * order // 128, 128), F32)],
        compiler_params=pltpu.CompilerParams(vmem_limit_bytes=12 << 20),
        cost_estimate=pl.CostEstimate(flops=6_000_000_000, bytes_accessed=3 << 20, transcendentals=0),
    )(where, own, other)


def factor_next(t, state):
    def body(w_in, l_in, i_in, w, l_ref, i_ref):
        factor_step(t, w, l_ref, i_ref)

    return pl.pallas_call(
        body,
        out_shape=tuple(jax.ShapeDtypeStruct(a.shape, F32) for a in state),
        in_specs=[VMEM] * 3,
        out_specs=(VMEM,) * 3,
        input_output_aliases={0: 0, 1: 1, 2: 2},
        compiler_params=pltpu.CompilerParams(vmem_limit_bytes=12 << 20),
        cost_estimate=pl.CostEstimate(flops=6_000_000_000, bytes_accessed=3 << 20, transcendentals=0),
    )(*state)


SLOTS = 3


def split(v):
    hi = v.astype(BF16)
    return hi, (v - hi.astype(F32)).astype(BF16)


def dot3(a, b, dim=0):
    def one(p, q):
        return lax.dot_general(p, q, (((1,), (dim,)), ((), ())), preferred_element_type=F32)

    return one(a[0], b[0]) + (one(a[0], b[1]) + one(a[1], b[0]))


def update_kernel(where, inv, near, far, own, *refs):
    pieces, (s_ref, new_ref, mine_ref), (pb, sb, ob, win, whi, wlo, psem, ssem, osem) = refs[:-12], refs[-12:-9], refs[-9:]
    y, x, c = where[1], where[2], where[3]
    count = len(pieces)

    def slab_part(ref, i, k):
        core, off = lax.rem(c + i // 4, NC), lax.rem(i, 4)
        yy = lax.rem(y + off + core * (k - off), NY)
        xx = lax.rem(x + k + core * (off - k), NX)
        return ref.at[:, yy, xx, core]

    def loads(i, slot, do):
        for k in range(NX):
            do(pltpu.make_async_copy(slab_part(s_ref, i, k), sb.at[slot, k], ssem.at[slot, k]))

    def piece_loads(i, slot, do):
        for n in range(count):
            parts = pieces[n]

            @pl.when(i == n)
            def _(parts=parts):
                at = 0
                for j, part in enumerate(parts):
                    size = part.shape[0]
                    do(pltpu.make_async_copy(part, pb.at[slot, pl.ds(at, size)], psem.at[slot, j]))
                    at += size

    def stores(i, slot, do):
        for k in range(NX):
            do(pltpu.make_async_copy(ob.at[slot, k], slab_part(new_ref, i, k), osem.at[slot, k]))

    def start(copy):
        copy.start()

    def wait(copy):
        copy.wait()

    for i in range(SLOTS - 1):
        loads(i, i, start)
        piece_loads(i, i, start)

    part = near.shape[1]
    for n in range(NZ):
        v = near[n] if n < NZ // 2 else far[n - NZ // 2]
        bits = n % 2 * 4 + n // 2 % 2 * 2 + n // 4
        win[pl.ds(pl.multiple_of((where[0] ^ bits) * part, part), part), :] = v
    inverse = split(inv[...])
    g = dot3(split(win[...]), inverse, 1)
    mine_ref[...] = dot3(split(own[...]), inverse, 1)
    w = dot3(split(g), inverse, 0).T
    whi[...], wlo[...] = split(w)

    @pl.loop(0, count)
    def _(i):
        slot = lax.rem(i, SLOTS)

        @pl.when(i + SLOTS - 1 < count)
        def _():
            later = lax.rem(i + SLOTS - 1, SLOTS)
            loads(i + SLOTS - 1, later, start)
            piece_loads(i + SLOTS - 1, later, start)

        loads(i, slot, wait)
        piece_loads(i, slot, wait)

        @pl.when(i >= SLOTS)
        def _():
            stores(i - SLOTS, slot, wait)

        got = dot3(split(pb[slot]), (whi[...], wlo[...]))
        rows = got.shape[0]
        old, new = sb.at[slot].reshape(2 * rows, 128), ob.at[slot].reshape(2 * rows, 128)
        for h in range(2):
            at = pl.ds(h, rows, stride=2)
            new[at, :] = old[at, :] - got[:, h * 128 : (h + 1) * 128]
        stores(i, slot, start)

    for i in range(count - SLOTS, count):
        stores(i, i % SLOTS, wait)


def update(where, inv, window, own, pieces, slab):
    flat = [a for parts in pieces for a in parts]
    sizes = [len(parts) for parts in pieces]
    cyc, rb, order = slab.shape[0], slab.shape[-2] // 2, inv.shape[0]
    width = slab.shape[-1] * 2

    def body(where, inv, near, far, own, *refs):
        grouped, at = [], 0
        for n in sizes:
            grouped.append(refs[at : at + n])
            at += n
        update_kernel(where, inv, near, far, own, *grouped, *refs[at:])

    return pl.pallas_call(
        body,
        out_shape=(jax.ShapeDtypeStruct(slab.shape, F32), jax.ShapeDtypeStruct(own.shape, F32)),
        in_specs=[SMEM, VMEM, VMEM, VMEM, VMEM] + [HBM] * (len(flat) + 1),
        out_specs=(HBM, VMEM),
        scratch_shapes=[
            pltpu.VMEM((SLOTS, NX * cyc * rb, order), F32),
            pltpu.VMEM((SLOTS, NX, cyc, 2 * rb, width // 2), F32),
            pltpu.VMEM((SLOTS, NX, cyc, 2 * rb, width // 2), F32),
            pltpu.VMEM((width, order), F32),
            pltpu.VMEM((order, width), BF16),
            pltpu.VMEM((order, width), BF16),
            pltpu.SemaphoreType.DMA((SLOTS, 2)),
            pltpu.SemaphoreType.DMA((SLOTS, NX)),
            pltpu.SemaphoreType.DMA((SLOTS, NX)),
        ],
        compiler_params=pltpu.CompilerParams(vmem_limit_bytes=14 << 20),
        cost_estimate=pl.CostEstimate(flops=5_000_000_000, bytes_accessed=26 << 20, transcendentals=0),
    )(where, inv, *window, own, *flat, slab)


def index(z, y, x, c):
    return ((z * NY + y) * NX + x) * NC + c


def receive(v, source):
    places = np.ndindex(NZ, NY, NX, NC)
    return lax.ppermute(v, ALL, [(index(*source(*at)), index(*at)) for at in places])


def along(phase, move):
    def source(z, y, x, c):
        return (z, y, move(x), c) if c == phase else (z, move(y), x, c)

    return source


def other_core(v):
    return receive(v, lambda z, y, x, c: (z, y, x, 1 - c))


def forward(up, down, phase):
    half = up.shape[0] // 2
    return [receive(down[:half], minus(phase)), receive(up[half:], plus(phase))]


def plus(phase):
    return along(phase, lambda i: (i + 1) % 4)


def minus(phase):
    return along(phase, lambda i: (i + 3) % 4)


def chip_rows(v, rows):
    core = lax.axis_index("core")
    got = other_core(v)
    return jnp.concatenate([jnp.where(core == 0, v[:rows], got[rows:]), jnp.where(core == 0, got[:rows], v[rows:])], 0)


def from_owner(v):
    return receive(v, lambda z, y, x, c: (y % 2 * NX + x, 2 * c + z // NX, z % NX, y // 2))


def everyone(v, axis, size):
    return lax.all_to_all(jnp.broadcast_to(v[None], (size, *v.shape)), axis, 0, 0, tiled=True)


def flip_z(b):
    return lambda z, y, x, c: (z ^ b, y, x, c)


def doubled(v, step):
    return jnp.concatenate([v, receive(v, step)], 0)


def local(diag_block, panel, slab):
    z, y, x, c = (lax.axis_index(a) for a in ALL)
    where = jnp.stack([z, y, x, c]).astype(jnp.int32)
    cyc, rb, order = panel.shape[0], panel.shape[-2], panel.shape[-1]
    p = own = panel.reshape(cyc * rb, order)
    tie = lax.optimization_barrier

    up, down = receive(p, plus(0)), receive(p, minus(0))
    d = everyone(diag_block.reshape(8, 128), "z", NZ)
    w = chip_rows(p[: 2 * rb], rb)
    d, up, down, w = tie((d, up, down, w))
    first, second = forward(up, down, 0)
    block = jnp.concatenate([p, up, first, second, down], 0)
    d = everyone(d, ("y", "x"), NY * NX).reshape(-1, 8, 128)
    w = from_owner(w).reshape(1, 2 * rb, order)
    d, block, w = tie((d, block, w))
    up, down = receive(block, plus(1)), receive(block, minus(1))
    state = factor_first(where, d, other_core(d), order)
    for t, bit in ((1, 4), (2, 2), (3, 1)):
        if t == 2:
            state, w, up, down = tie((state, w, up, down))
            first, second = forward(up, down, 1)
        else:
            state, w = tie((state, w))
        got = receive(w, flip_z(bit))
        state = factor_next(t, state)
        if bit > 1:
            w = jnp.concatenate([w, got], 0)
    _, factor, inverse = state
    window = (w, got)
    pieces = [[block], [up], [first, second], [down]]
    pieces += [[other_core(a) for a in parts] for parts in pieces]

    view = slab.reshape(cyc, NY, NX, NC, 2 * rb, slab.shape[-1] // 2)
    new, mine = update(where, inverse, window, own, pieces, view)
    rows = diag_block.shape[0]
    own_factor = lax.dynamic_slice_in_dim(factor, index(z, y, x, c) * rows, rows, 0)
    return own_factor, mine.reshape(panel.shape), new.reshape(slab.shape)


def solution(mesh):
    fine = Mesh(np.asarray(mesh.devices).reshape(NZ, NY, NX, NC), ALL)
    placed = (
        P(ALL, None),
        P(None, "z", ("y", "x", "core"), None, None),
        P(None, "z", None, ("y", "x", "core"), None),
    )
    return jax.shard_map(local, mesh=fine, in_specs=placed, out_specs=placed, check_vma=False)
```
